256 devices in a mesh: rep: 32 (over z_hi, y, core), fsdp: 8 (over z_lo, x).
Axes of the slice: x: 4, y: 4, z: 8 (z_hi: 4, z_lo: 2; z = z_hi * 2 + z_lo), core: 2. Of those that a mesh axis runs over, the one named last changes fastest.
Arguments:
- inputs: bfloat16 [32, 2, 2048, 4096], P('rep', None, 'fsdp'), may hold values from -6 to 6
- queries: bfloat16 [32, 2, 2048, 4096], P('rep', None, 'fsdp'), may hold values from -6 to 6
- keys: bfloat16 [32, 2, 2048, 512], P('rep', None, 'fsdp'), may hold values from -6 to 6
- value_w: bfloat16 [32, 512, 4096], P('rep', None, 'fsdp'), may hold values from -0.09375 to 0.09375
- anchor: float32 [512, 4096], P('rep', 'fsdp'), may hold values from -0.09375 to 0.09375
- momentum: float32 [512, 4096], P('rep', 'fsdp'), may hold values from -0.3 to 0.3
- prev_delta: bfloat16 [32, 512, 4096], P('rep', None, 'fsdp'), may hold values from -1.1953125 to 1.1953125
Outputs:
- value_out: bfloat16 [32, 512, 4096], P('rep', None, 'fsdp')
- anchor_out: float32 [512, 4096], P('rep', 'fsdp')
- momentum_out: float32 [512, 4096], P('rep', 'fsdp')
- delta_out: bfloat16 [32, 512, 4096], P('rep', None, 'fsdp')
The draws below stay inside these ranges and needn't reach their ends.
All inputs are finite; a program needn't handle non-finite values.
Results may differ from the reference program's by a relative error of at most 0.029.
Values may be sent and summed in bfloat16 or wider, within the bound.
No kernel may reach another device: no remote copies, remote signals or barrier semaphores. Data moves between devices by JAX's collectives and lax.ppermute only.
A program may use at most 128 MiB of HBM per device.

```python
import math
import jax
import jax.numpy as jnp
from jax import lax

D = 4096
HD = 128
HQ = 32
KVH = 4
STEPS = 2
TOK_DEV = 256
KV = 512
TOKENS = 2048
REPS = 32
N_FSDP = 8


def draw_keys(key, part):
    key = jax.random.fold_in(key, 11)
    return jnp.clip(jax.random.normal(key, (REPS, STEPS, TOKENS, KVH * HD)), -6.0, 6.0).astype(jnp.bfloat16)


def draw_queries(key, part):
    key = jax.random.fold_in(key, 13)
    return jnp.clip(jax.random.normal(key, (REPS, STEPS, TOKENS, HQ * HD)), -6.0, 6.0).astype(jnp.bfloat16)


def with_spikes(entries, rng, source, target, shards_of, factor):
    owner, partner = [(jnp.arange(entries.shape[axis_at]) // (entries.shape[axis_at] // shards_of)).reshape([-1 if axis == axis_at else 1 for axis in range(entries.ndim)]) for axis_at in (source, target)]
    chosen = jax.random.permutation(rng, shards_of)[partner]
    strong = (owner == chosen) | (owner == (partner + shards_of // 2) % shards_of)
    return jnp.where(strong, factor * entries, entries)


def level_of(own_key, shape, cuts, low, largest):
    gain, own = 1.0, jax.random.fold_in(own_key, 6)
    for axis_at, shards_of in cuts:
        draws = jnp.exp(jax.random.uniform(jax.random.fold_in(own, axis_at), (shards_of,), jnp.float32, low / len(cuts), largest / len(cuts)))
        gain = gain * jnp.repeat(draws, shape[axis_at] // shards_of).reshape([-1 if axis == axis_at else 1 for axis in range(len(shape))])
    return gain


def bell_draw(own_key, dims, scale, bound, pieces=(), kind=jnp.bfloat16):
    factor_of = level_of(own_key, dims, pieces, -0.22, 0.18) if pieces else 1.0
    result = jax.random.normal(own_key, dims, jnp.float32) * scale * factor_of
    return jnp.minimum(jnp.maximum(result, -bound), bound).astype(kind)


def heavy_noise(stream_key, dims, deviation, most, split, heavy, dtype=jnp.bfloat16):
    array = deviation * jax.random.normal(stream_key, dims, jnp.float32)
    if split:
        array = array * level_of(stream_key, dims, split, -0.22, 0.18)
    return jnp.clip(with_spikes(array, jax.random.fold_in(stream_key, 3), *heavy), -most, most).astype(dtype)


def setup_inputs(seed: int = 0) -> dict:
    streams_of = jax.random.split(jax.random.key(seed), 8)
    return {
        "inputs": bell_draw(streams_of[0], (REPS, STEPS, TOKENS, D), 1.0, 6.0, ((0, 32), (2, 8))),
        "queries": draw_queries(jax.random.fold_in(streams_of[7], 71), 0),
        "keys": draw_keys(jax.random.fold_in(streams_of[7], 71), 0),
        "value_w": bell_draw(streams_of[3], (REPS, KV, D), D ** -0.5, 0.09375, ((0, 32), (2, 8))),
        "anchor": bell_draw(streams_of[4], (KV, D), D ** -0.5, 0.09375, ((0, 32), (1, 8)), jnp.float32),
        "momentum": bell_draw(streams_of[5], (KV, D), 0.05, 0.3, ((0, 32), (1, 8)), jnp.float32),
        "prev_delta": heavy_noise(streams_of[6], (REPS, KV, D), 0.2, 1.1953125, ((0, 32), (2, 8)), (0, 1, 32, 2.75)),
    }


inner_rate = 0.5
outer_rate = 0.7
outer_mu = 0.9
mix_share = 0.5

def block_sum(left, right):
    left_blocks = left.reshape(N_FSDP, -1, left.shape[1]).astype(jnp.float32)
    right_blocks = right.reshape(N_FSDP, -1, right.shape[1]).astype(jnp.float32)
    partial_sums = jnp.einsum('btl,btr->blr', left_blocks, right_blocks).astype(jnp.bfloat16)
    partial_sums = lax.optimization_barrier(partial_sums)
    return lax.optimization_barrier(jnp.sum(partial_sums.astype(jnp.float32), axis=0))

def attend(query_rows, key_rows, value_rows):
    seq_count = query_rows.shape[0] // TOK_DEV
    group_size = HQ // KVH
    query_heads = query_rows.reshape(seq_count, TOK_DEV, KVH, group_size, HD).astype(jnp.float32)
    key_heads = key_rows.reshape(seq_count, TOK_DEV, KVH, HD).astype(jnp.float32)
    scores = jnp.einsum('btkgd,bukd->bkgtu', query_heads, key_heads) * (1.0 / math.sqrt(HD))
    causal = jnp.arange(TOK_DEV)[:, None] >= jnp.arange(TOK_DEV)[None, :]
    scores = jnp.where(causal, scores, -1e+30)
    peak_score = lax.optimization_barrier(jnp.max(scores, axis=-1, keepdims=True))
    expons = jnp.exp(scores - peak_score)
    weights_bf = (expons / lax.optimization_barrier(jnp.sum(expons, axis=-1, keepdims=True))).astype(jnp.bfloat16)
    value_heads = value_rows.reshape(seq_count, TOK_DEV, KVH, HD).astype(jnp.float32)
    output = jnp.einsum('bkgtu,bukd->btkgd', weights_bf.astype(jnp.float32), value_heads)
    return (weights_bf, output.reshape(seq_count * TOK_DEV, HQ * HD))

def value_gradient(weights_bf, grad_out):
    seq_count = grad_out.shape[0] // TOK_DEV
    group_size = HQ // KVH
    grad_heads = grad_out.reshape(seq_count, TOK_DEV, KVH, group_size, HD).astype(jnp.float32)
    grad_value = jnp.einsum('bkgtu,btkgd->bukd', weights_bf.astype(jnp.float32), grad_heads)
    return grad_value.reshape(seq_count * TOK_DEV, KVH * HD).astype(jnp.bfloat16)

def one_replica(packed):
    rows_all, query_all, key_all, value_now = packed
    for inner_step in range(STEPS):
        token_rows = rows_all[inner_step]
        value_rows = jnp.dot(token_rows, value_now.T, preferred_element_type=jnp.float32).astype(jnp.bfloat16)
        weights_bf, output = attend(query_all[inner_step], key_all[inner_step], value_rows)
        blocks = token_rows.reshape(-1, TOK_DEV, D)
        target = jnp.concatenate([blocks[:, 1:], jnp.zeros((blocks.shape[0], 1, D), jnp.bfloat16)], axis=1)
        target = target.reshape(-1, D).astype(jnp.float32)
        grad_out = (output - target).astype(jnp.bfloat16)
        grad_value = value_gradient(weights_bf, grad_out)
        sum_value = block_sum(grad_value, token_rows)
        value_now = (value_now.astype(jnp.float32) - inner_rate * (1.0 / TOKENS) * sum_value).astype(jnp.bfloat16)
    return value_now

def reference(inputs, queries, keys, value_w, anchor, momentum, prev_delta):
    inner_value = lax.map(one_replica, (inputs, queries, keys, value_w))
    average = lax.optimization_barrier(jnp.sum(prev_delta.astype(jnp.float32), axis=0)) / REPS
    momentum_out = outer_mu * momentum + average
    anchor_out = anchor - outer_rate * (outer_mu * momentum_out + average)
    inner_float = inner_value.astype(jnp.float32)
    value_out = (mix_share * inner_float + (1.0 - mix_share) * anchor_out[None]).astype(jnp.bfloat16)
    delta_out = (anchor[None] - inner_float).astype(jnp.bfloat16)
    return (value_out, anchor_out, momentum_out, delta_out)
```

```python
import functools
import math

import jax
import jax.numpy as jnp
from jax import lax
from jax.experimental import pallas as pl
from jax.experimental.pallas import tpu as pltpu
from jax.sharding import PartitionSpec as P

HD = 128
HQ = 32
KVH = 4
GROUP = HQ // KVH
STEPS = 2
CHUNKS = 2
NX = 4
NZ = 2
NY = 4
NZH = 4

inner_rate = 0.5
outer_rate = 0.7
outer_mu = 0.9
mix_share = 0.5

BF = jnp.bfloat16
F32 = jnp.float32
NT = (((1,), (1,)), ((), ()))
NN = (((1,), (0,)), ((), ()))
VMEM_LIMIT = 16 * 1024 * 1024
COST = pl.CostEstimate(flops=1000, bytes_accessed=1000, transcendentals=0)

X_PLUS = [(i, i // NX * NX + (i % NX + 1) % NX) for i in range(NX * NZ)]
X_MINUS = [(i, i // NX * NX + (i % NX + NX - 1) % NX) for i in range(NX * NZ)]
Z_SWAP = [(i, (i + NX) % (NX * NZ)) for i in range(NX * NZ)]
N_REP = NZH * NY * 2
CORE_SWAP = [(r, r ^ 1) for r in range(N_REP)]


def y_shift(d):
    return [(r, r // 8 * 8 + (r // 2 % NY + d) % NY * 2 + r % 2) for r in range(N_REP)]


def zh_shift(d):
    return [(r, (r // 8 + d) % NZH * 8 + r % 8) for r in range(N_REP)]


def dot(a, b, dims):
    return lax.dot_general(a, b, dims, preferred_element_type=F32)


def attention_kernel(q_ref, k_ref, x_ref, m_ref, nt_ref, w_low, w_high, targets):
    length = k_ref.shape[0]
    half = length // 2
    k_low, k_high = k_ref[:half, :], k_ref[half:, :]
    u_at = lax.broadcasted_iota(jnp.int32, (half, half), 0)
    t_at = lax.broadcasted_iota(jnp.int32, (half, half), 1)
    keep = u_at <= t_at
    row_at = lax.broadcasted_iota(jnp.int32, (length, HD), 0)
    factor = math.log2(math.e) / math.sqrt(HD)
    for g in range(GROUP):
        cols = slice(g * HD, (g + 1) * HD)
        q_low, q_high = q_ref[:half, cols], q_ref[half:, cols]
        s_low = jnp.where(keep, dot(k_low, q_low, NT), -1e30)
        s_top = dot(k_low, q_high, NT)
        s_diag = jnp.where(keep, dot(k_high, q_high, NT), -1e30)
        peak = jnp.max(s_low, axis=0, keepdims=True)
        e_low = jnp.exp2((s_low - peak) * factor)
        w_low[:, cols] = (e_low * (1.0 / jnp.sum(e_low, axis=0, keepdims=True))).astype(BF)
        peak = jnp.max(jnp.maximum(s_top, s_diag), axis=0, keepdims=True)
        e_top = jnp.exp2((s_top - peak) * factor)
        e_diag = jnp.exp2((s_diag - peak) * factor)
        share = 1.0 / jnp.sum(e_top + e_diag, axis=0, keepdims=True)
        w_high[:half, cols] = (e_top * share).astype(BF)
        w_high[half:, cols] = (e_diag * share).astype(BF)
        shifted = pltpu.roll(x_ref[:, cols].astype(F32), length - 1, 0)
        target = jnp.where(row_at == length - 1, 0.0, shifted).astype(BF)
        targets[0, g * half : (g + 1) * half, :] = target[:half]
        targets[1, g * half : (g + 1) * half, :] = target[half:]
    m_high = dot(w_high[...], w_high[...], NT)
    m_low = dot(w_low[...], w_low[...], NT)
    m_ref[:half, :half] = (m_high[:half, :half] + m_low).astype(BF)
    m_ref[:half, half:] = m_high[:half, half:].astype(BF)
    m_ref[half:, :] = m_high[half:, :].astype(BF)
    n_high = dot(w_high[...], targets[1], NN)
    n_low = dot(w_low[...], targets[0], NN)
    nt_ref[:, :half] = (n_high[:half] + n_low).T
    nt_ref[:, half:] = n_high[half:].T


def attention_matrices(queries, keys, rows, step):
    length = rows.shape[2]
    half = length // 2
    wide = GROUP * HD
    return pl.pallas_call(
        attention_kernel,
        grid=(KVH,),
        in_specs=[
            pl.BlockSpec((None, None, length, wide), lambda j: (0, step, 0, j)),
            pl.BlockSpec((None, None, length, HD), lambda j: (0, step, 0, j)),
            pl.BlockSpec((None, None, length, wide), lambda j: (0, step, 0, j)),
        ],
        out_specs=[
            pl.BlockSpec((None, length, length), lambda j: (j, 0, 0)),
            pl.BlockSpec((HD, length), lambda j: (j, 0)),
        ],
        out_shape=[
            jax.ShapeDtypeStruct((KVH, length, length), BF),
            jax.ShapeDtypeStruct((KVH * HD, length), F32),
        ],
        scratch_shapes=[
            pltpu.VMEM((half, GROUP * half), BF),
            pltpu.VMEM((length, GROUP * half), BF),
            pltpu.VMEM((2, GROUP * half, HD), BF),
        ],
        compiler_params=pltpu.CompilerParams(vmem_limit_bytes=VMEM_LIMIT),
        cost_estimate=COST,
        name="attention_matrices",
    )(queries, keys, rows)


VMEM = pl.BlockSpec(memory_space=pltpu.VMEM)
SMEM = pl.BlockSpec(memory_space=pltpu.SMEM)


def own_columns(x_id, k, width):
    return pl.ds(pl.multiple_of((x_id + k) % NX * width, width), width)


def value_kernel(first, x_at, own, left, right, opp, mine, other, keep_ref, send_ref):
    n_kv, width = opp.shape
    rows = slice(first, first + n_kv)
    parts = [(own[rows, :], 0), (right[rows, :], 1), (opp[...], 2), (left[rows, :], 3)]
    for src, dst in ((other, send_ref), (mine, keep_ref)):
        acc = None
        for w_part, k in parts:
            term = dot(w_part, src[:, own_columns(x_at[0], k, width)], NT)
            acc = term if acc is None else acc + term
        dst[...] = acc.astype(dst.dtype)


def value_partial(x_id, first, pieces, mine, other):
    n_kv, length = pieces[3].shape[0], mine.shape[0]
    return pl.pallas_call(
        functools.partial(value_kernel, first),
        in_specs=[SMEM] + [VMEM] * 6,
        out_specs=[VMEM] * 2,
        out_shape=[
            jax.ShapeDtypeStruct((n_kv, length), F32),
            jax.ShapeDtypeStruct((n_kv, length), BF),
        ],
        compiler_params=pltpu.CompilerParams(vmem_limit_bytes=VMEM_LIMIT),
        cost_estimate=COST,
        name="value_partial",
    )(x_id, *pieces, mine, other)


def grad_kernel(first, keep, got, m_ref, nt_ref, out):
    value = (keep[...] + got[...].astype(F32)).astype(BF)
    for j in range(out.shape[0] // HD):
        rows = slice(j * HD, (j + 1) * HD)
        at = first + j
        minus = nt_ref[at * HD : (at + 1) * HD, :]
        out[rows, :] = (dot(value[rows, :], m_ref[at], NN) - minus).astype(BF)


def grad_value(keep, got, m_all, nt_all, first):
    return pl.pallas_call(
        functools.partial(grad_kernel, first // HD),
        in_specs=[VMEM] * 4,
        out_specs=VMEM,
        out_shape=jax.ShapeDtypeStruct(keep.shape, BF),
        compiler_params=pltpu.CompilerParams(vmem_limit_bytes=VMEM_LIMIT),
        cost_estimate=COST,
        name="grad_value",
    )(keep, got, m_all, nt_all)


def sum_kernel(side, x_at, g_mine, g_other, mine, other, opp, plain, own, added):
    width = own.shape[1]
    for k, dst in ((2, opp), (4 - side, plain), (side, added), (0, own)):
        cols = own_columns(x_at[0], k, width)
        term = dot(g_mine[...], mine[:, cols], NN) + dot(g_other[...], other[:, cols], NN)
        dst[...] = term.astype(dst.dtype)


def sum_partial(x_id, side, g_mine, g_other, mine, other):
    n_kv, width = g_mine.shape[0], mine.shape[1] // NX
    return pl.pallas_call(
        functools.partial(sum_kernel, side),
        in_specs=[SMEM] + [VMEM] * 4,
        out_specs=[VMEM] * 4,
        out_shape=[
            jax.ShapeDtypeStruct((n_kv, width), BF),
            jax.ShapeDtypeStruct((n_kv, width), BF),
            jax.ShapeDtypeStruct((n_kv, width), F32),
            jax.ShapeDtypeStruct((n_kv, width), F32),
        ],
        compiler_params=pltpu.CompilerParams(vmem_limit_bytes=VMEM_LIMIT),
        cost_estimate=COST,
        name="sum_partial",
    )(x_id, g_mine, g_other, mine, other)


def send(value, perm):
    return lax.ppermute(value, "fsdp", perm)


def after(value, *others):
    return lax.optimization_barrier((value, *others))[0]


def gather_x(side, own):
    left = send(own, X_PLUS)
    right = send(own, X_MINUS)
    opp = send(left, X_PLUS) if side == 1 else send(right, X_MINUS)
    return own, left, right, opp


def reduce_x(side, opp, plain, own, added):
    there, back = (X_PLUS, X_MINUS) if side == 1 else (X_MINUS, X_PLUS)
    opp_in = send(opp, there)
    plain_in = send(plain, back)
    added_in = send((added + opp_in.astype(F32)).astype(BF), there)
    return own + plain_in.astype(F32) + added_in.astype(F32)


def inner_steps(inputs, queries, keys, value_w):
    length, width = inputs.shape[2:]
    half_width = width // NZ
    at = lax.axis_index("fsdp")
    x_id = (at % NX).astype(jnp.int32).reshape(1)
    z_id = at // NX
    scale_rows = 1.0 / (length * NX * NZ)
    n_kv = value_w.shape[1] // CHUNKS
    firsts = [c * n_kv for c in range(CHUNKS)]
    sides = [1, 3]

    def columns(rows, step, half):
        start = (0, step, 0, half * half_width)
        return lax.dynamic_slice(rows, start, (1, 1, length, half_width))[0, 0]

    away = columns(inputs, 0, 1 - z_id)
    other = send(away, Z_SWAP)
    w_own = value_w[0]
    w_left, w_right = send(w_own, X_PLUS), send(w_own, X_MINUS)
    w_opp = [send(w_left[:n_kv], X_PLUS), send(w_right[n_kv:], X_MINUS)]
    gathered = [(w_own, w_left, w_right, w_opp[c]) for c in range(CHUNKS)]
    offsets = firsts
    mine = columns(after(inputs, away), 0, z_id)
    matrices = [attention_matrices(after(queries, away), keys, inputs, 0)]
    gate = matrices[0][1]
    matrices.append(attention_matrices(after(queries, gate), keys, inputs, 1))
    w_now = [w_own[f : f + n_kv] for f in firsts]
    for step in range(STEPS):
        m_all, nt_all = matrices[step]
        partials = [value_partial(x_id, o, g, mine, other) for o, g in zip(offsets, gathered)]
        got = [send(p[1], Z_SWAP) for p in partials]
        g_mine = [grad_value(p[0], got[c], m_all, nt_all, firsts[c]) for c, p in enumerate(partials)]
        g_other = [send(g, Z_SWAP) for g in g_mine]
        if step + 1 < STEPS:
            later = after(inputs, matrices[-1][1])
            next_mine = columns(later, step + 1, z_id)
            away = columns(later, step + 1, 1 - z_id)
            away, g_other[-1] = lax.optimization_barrier((away, g_other[-1]))
            next_other = send(away, Z_SWAP)
        for c in range(CHUNKS):
            parts = sum_partial(x_id, sides[c], g_mine[c], g_other[c], mine, other)
            sums = reduce_x(sides[c], *parts)
            w_now[c] = (w_now[c].astype(F32) - inner_rate * scale_rows * sums).astype(BF)
        if step + 1 < STEPS:
            mine, other = next_mine, next_other
            gathered = [gather_x(sides[c], w_now[c]) for c in range(CHUNKS)]
            offsets = [0] * CHUNKS
    return jnp.concatenate(w_now, axis=0), gate


def turn(items, shift):
    count = len(items)
    twice = jnp.stack(list(items) + list(items[:-1]), axis=0)
    return lax.dynamic_slice_in_dim(twice, (count - shift) % count, count, 0)


def take(array, index, axis):
    return lax.dynamic_index_in_dim(array, index, axis, keepdims=False)


def outer_update(anchor, momentum, prev_delta):
    height, width = anchor.shape
    rep = lax.axis_index("rep")
    z_hi, y_at, core = rep // 8, rep // 2 % NY, rep % 2

    def hop(value, perm):
        return lax.ppermute(value, "rep", perm)

    parts = prev_delta[0].reshape(NZH * NY, 2, height, width)
    got = hop(take(parts, 1 - core, 1), CORE_SWAP)
    sums = take(parts, core, 1).astype(F32) + got.astype(F32)
    sums = sums.reshape(NZH, NY, height, width)
    small = sums.astype(BF)
    total = take(sums, y_at, 1)
    for d in (1, 2, 3):
        total = total + hop(take(small, (y_at + d) % NY, 1), y_shift(d)).astype(F32)
    small = total.astype(BF)
    last = take(total, z_hi, 0)
    for d in (1, 2, 3):
        last = last + hop(take(small, (z_hi + d) % NZH, 0), zh_shift(d)).astype(F32)
    average = last / N_REP
    momentum_out = outer_mu * momentum + average
    anchor_out = anchor - outer_rate * (outer_mu * momentum_out + average)
    both = jnp.stack([anchor_out.astype(BF), anchor.astype(BF)], axis=0)
    near = [both] + [hop(both, zh_shift(NZH - d)) for d in (1, 2, 3)]
    both = turn(near, z_hi)
    near = [both] + [hop(both, y_shift(NY - d)) for d in (1, 2, 3)]
    both = turn(near, y_at)
    both = turn([both, hop(both, CORE_SWAP)], core)
    both = both.transpose(3, 2, 1, 0, 4, 5).reshape(2, N_REP * height, width)
    return both[1], both[0], momentum_out, anchor_out


def shards(inputs, queries, keys, value_w, anchor, momentum, prev_delta):
    value_now, gate = inner_steps(inputs, queries, keys, value_w)
    outer_parts = outer_update(anchor, momentum, after(prev_delta, gate))
    anchor_full, anchor_new, momentum_out, anchor_out = outer_parts
    inner_float = value_now.astype(F32)
    value_out = (mix_share * inner_float + (1.0 - mix_share) * anchor_new.astype(F32)).astype(BF)
    delta_out = (anchor_full.astype(F32) - inner_float).astype(BF)
    return (value_out[None], anchor_out, momentum_out, delta_out[None])


def solution(mesh):
    placed = (
        P("rep", None, "fsdp", None),
        P("rep", None, "fsdp", None),
        P("rep", None, "fsdp", None),
        P("rep", None, "fsdp"),
        P("rep", "fsdp"),
        P("rep", "fsdp"),
        P("rep", None, "fsdp"),
    )
    return jax.shard_map(
        shards,
        mesh=mesh,
        in_specs=placed,
        out_specs=(
            P("rep", None, "fsdp"),
            P("rep", "fsdp"),
            P("rep", "fsdp"),
            P("rep", None, "fsdp"),
        ),
        check_vma=False,
    )
```

```python
import functools
import math

import jax
import jax.numpy as jnp
from jax import lax
from jax.experimental import pallas as pl
from jax.experimental.pallas import tpu as pltpu
from jax.sharding import PartitionSpec as P

HD = 128
HQ = 32
KVH = 4
GROUP = HQ // KVH
STEPS = 2
CHUNKS = 2
NX = 4
NZ = 2

inner_rate = 0.5
outer_rate = 0.7
outer_mu = 0.9
mix_share = 0.5

BF = jnp.bfloat16
F32 = jnp.float32
NT = (((1,), (1,)), ((), ()))
NN = (((1,), (0,)), ((), ()))
VMEM_LIMIT = 16 * 1024 * 1024
ATTENTION_LIMIT = 60 * 1024 * 1024
TOKEN = ((8, 128), F32)
COST = pl.CostEstimate(flops=1000, bytes_accessed=1000, transcendentals=0)

X_PLUS = [(i, i // NX * NX + (i % NX + 1) % NX) for i in range(NX * NZ)]
X_MINUS = [(i, i // NX * NX + (i % NX + NX - 1) % NX) for i in range(NX * NZ)]
Z_SWAP = [(i, (i + NX) % (NX * NZ)) for i in range(NX * NZ)]
NY = 4
NZH = 4
N_REP = NZH * NY * 2


def dot(a, b, dims):
    return lax.dot_general(a, b, dims, preferred_element_type=F32)


def attention_kernel(_, t_in, q_ref, k_ref, x_ref, m_ref, nt_ref, t_out, w_low, w_high, targets):
    t_out[...] = t_in[...]
    length = k_ref.shape[0]
    half = length // 2
    k_low, k_high = k_ref[:half, :], k_ref[half:, :]
    u_at = lax.broadcasted_iota(jnp.int32, (half, half), 0)
    t_at = lax.broadcasted_iota(jnp.int32, (half, half), 1)
    keep = u_at <= t_at
    row_at = lax.broadcasted_iota(jnp.int32, (length, HD), 0)
    factor = math.log2(math.e) / math.sqrt(HD)
    for g in range(GROUP):
        cols = slice(g * HD, (g + 1) * HD)
        q_low, q_high = q_ref[:half, cols], q_ref[half:, cols]
        s_low = jnp.where(keep, dot(k_low, q_low, NT), -1e30)
        s_top = dot(k_low, q_high, NT)
        s_diag = jnp.where(keep, dot(k_high, q_high, NT), -1e30)
        peak = jnp.max(s_low, axis=0, keepdims=True)
        e_low = jnp.exp2((s_low - peak) * factor)
        w_low[:, cols] = (e_low * (1.0 / jnp.sum(e_low, axis=0, keepdims=True))).astype(BF)
        peak = jnp.max(jnp.maximum(s_top, s_diag), axis=0, keepdims=True)
        e_top = jnp.exp2((s_top - peak) * factor)
        e_diag = jnp.exp2((s_diag - peak) * factor)
        share = 1.0 / jnp.sum(e_top + e_diag, axis=0, keepdims=True)
        w_high[:half, cols] = (e_top * share).astype(BF)
        w_high[half:, cols] = (e_diag * share).astype(BF)
        shifted = pltpu.roll(x_ref[:, cols].astype(F32), length - 1, 0)
        target = jnp.where(row_at == length - 1, 0.0, shifted).astype(BF)
        targets[0, g * half : (g + 1) * half, :] = target[:half]
        targets[1, g * half : (g + 1) * half, :] = target[half:]
    m_high = dot(w_high[...], w_high[...], NT)
    m_low = dot(w_low[...], w_low[...], NT)
    m_ref[:half, :half] = (m_high[:half, :half] + m_low).astype(BF)
    m_ref[:half, half:] = m_high[:half, half:].astype(BF)
    m_ref[half:, :] = m_high[half:, :].astype(BF)
    n_high = dot(w_high[...], targets[1], NN)
    n_low = dot(w_low[...], targets[0], NN)
    nt_ref[:, :half] = (n_high[:half] + n_low).T
    nt_ref[:, half:] = n_high[half:].T


def attention_matrices(before, token, queries, keys, rows, step):
    length = rows.shape[2]
    half = length // 2
    wide = GROUP * HD
    m_part, nt_part, token = pl.pallas_call(
        attention_kernel,
        grid=(KVH,),
        in_specs=[
            pl.BlockSpec(memory_space=pl.ANY),
            pl.BlockSpec(TOKEN[0], lambda j: (0, 0)),
            pl.BlockSpec((None, None, length, wide), lambda j: (0, step, 0, j)),
            pl.BlockSpec((None, None, length, HD), lambda j: (0, step, 0, j)),
            pl.BlockSpec((None, None, length, wide), lambda j: (0, step, 0, j)),
        ],
        out_specs=[
            pl.BlockSpec((None, length, length), lambda j: (j, 0, 0)),
            pl.BlockSpec((HD, length), lambda j: (j, 0)),
            pl.BlockSpec(TOKEN[0], lambda j: (0, 0)),
        ],
        out_shape=[
            jax.ShapeDtypeStruct((KVH, length, length), BF),
            jax.ShapeDtypeStruct((KVH * HD, length), F32),
            jax.ShapeDtypeStruct(*TOKEN),
        ],
        scratch_shapes=[
            pltpu.VMEM((half, GROUP * half), BF),
            pltpu.VMEM((length, GROUP * half), BF),
            pltpu.VMEM((2, GROUP * half, HD), BF),
        ],
        compiler_params=pltpu.CompilerParams(vmem_limit_bytes=ATTENTION_LIMIT),
        cost_estimate=COST,
        name="attention_matrices",
    )(before, token, queries, keys, rows)
    return (m_part, nt_part), token


VMEM = pl.BlockSpec(memory_space=pltpu.VMEM)
SMEM = pl.BlockSpec(memory_space=pltpu.SMEM)


def ordered(body, name, x_id, token, operands, outs):
    def kernel(x_at, token_in, *refs):
        body(x_at[0], *refs[:-1])
        refs[-1][...] = token_in[...]

    results = pl.pallas_call(
        kernel,
        in_specs=[SMEM] + [VMEM] * (1 + len(operands)),
        out_specs=[VMEM] * (len(outs) + 1),
        out_shape=[jax.ShapeDtypeStruct(*o) for o in [*outs, TOKEN]],
        compiler_params=pltpu.CompilerParams(vmem_limit_bytes=VMEM_LIMIT),
        cost_estimate=COST,
        name=name,
    )(x_id, token, *operands)
    return results[:-1], results[-1]


def own_columns(x_id, k, width):
    return pl.ds(pl.multiple_of((x_id + k) % NX * width, width), width)


def value_piece(x_id, own, left, right, opp, rows):
    width = own.shape[1]
    acc = None
    for w_part, k in ((own, 0), (right, 1), (opp, 2), (left, 3)):
        term = dot(w_part[...], rows[:, own_columns(x_id, k, width)], NT)
        acc = term if acc is None else acc + term
    return acc


def value_body(x_id, own, left, right, opp, *refs):
    out, first = refs[-1], 0
    for other in refs[:-1]:
        cols = slice(first, first + other.shape[0])
        out[:, cols] = value_piece(x_id, own, left, right, opp, other).astype(BF)
        first = cols.stop


def grad_body(first, x_id, own, left, right, opp, mine, got, m_ref, nt_ref, out):
    value = value_piece(x_id, own, left, right, opp, mine)
    value = (value + got[...].astype(F32)).astype(BF)
    for j in range(out.shape[0] // HD):
        rows = slice(j * HD, (j + 1) * HD)
        at = first + j
        minus = nt_ref[at * HD : (at + 1) * HD, :]
        out[rows, :] = (dot(value[rows, :], m_ref[at], NN) - minus).astype(BF)


def sum_piece(x_id, k, width, g_mine, g_other, rows):
    cols = own_columns(x_id, k, width)
    total = dot(g_mine[...], rows[0][:, cols], NN)
    first = 0
    for other in rows[1:]:
        tokens = slice(first, first + other.shape[0])
        total = total + dot(g_other[:, tokens], other[:, cols], NN)
        first = tokens.stop
    return total


def sum_body(side, x_id, g_mine, g_other, *refs):
    *rows, opp, plain = refs
    width = opp.shape[1]
    for k, dst in ((2, opp), (4 - side, plain)):
        dst[...] = sum_piece(x_id, k, width, g_mine, g_other, rows).astype(BF)


def add_body(side, x_id, g_mine, g_other, *refs):
    *rows, opp_in, out = refs
    term = sum_piece(x_id, side, out.shape[1], g_mine, g_other, rows)
    out[...] = (term + opp_in[...].astype(F32)).astype(BF)


def step_body(rate, x_id, g_mine, g_other, *refs):
    *rows, plain_in, added_in, w_ref, out = refs
    total = sum_piece(x_id, 0, out.shape[1], g_mine, g_other, rows)
    total = total + plain_in[...].astype(F32) + added_in[...].astype(F32)
    out[...] = (w_ref[...].astype(F32) - rate * total).astype(BF)


def own_body(x_id, g_mine, g_other, *refs):
    *rows, out = refs
    out[...] = sum_piece(x_id, 0, out.shape[1], g_mine, g_other, rows)


def last_body(rate, n, x_id, *refs):
    *rows_refs, both, value_out, delta_out = refs[5 * n :]
    n_kv, (n_y, _, n_z, height, _) = value_out.shape[1] // n, both.shape
    near = [[both[y, i, z] for z in range(n_z) for y in range(n_y)] for i in (0, 1)]
    for c in range(n):
        g_mine, g_other, plain_in, added_in, w_ref = refs[5 * c : 5 * c + 5]
        total = sum_piece(x_id, 0, w_ref.shape[1], g_mine, g_other, rows_refs)
        total = total + plain_in[...].astype(F32) + added_in[...].astype(F32)
        inner = (w_ref[...].astype(F32) - rate * total).astype(BF).astype(F32)
        rows = slice(c * n_kv, (c + 1) * n_kv)
        here = slice(c * n_kv // height, (c + 1) * n_kv // height)
        new, old = (jnp.concatenate(v[here], axis=0).astype(F32) for v in near)
        value_out[0, rows, :] = (mix_share * inner + (1.0 - mix_share) * new).astype(BF)
        delta_out[0, rows, :] = (old - inner).astype(BF)


def send(value, perm):
    return lax.ppermute(value, "fsdp", perm)


def gather_x(side, own, gate=None):
    left = send(own, X_PLUS)
    right = send(own, X_MINUS)
    near, perm = (left, X_PLUS) if side == 1 else (right, X_MINUS)
    return own, left, right, send(near if gate is None else gated(near, gate), perm)


def gated(value, token):
    return lax.optimization_barrier((value, token))[0]


def inner_steps(inputs, queries, keys, value_w, outer):
    length, width = inputs.shape[2:]
    half_width = width // NZ
    at = lax.axis_index("fsdp")
    x_id = (at % NX).astype(jnp.int32).reshape(1)
    z_id = at // NX
    rate = inner_rate / (length * NX * NZ)
    n_kv = value_w.shape[1] // CHUNKS
    firsts = [c * n_kv for c in range(CHUNKS)]
    sides = [1, 3]
    chunks = range(CHUNKS)
    there = [X_PLUS, X_MINUS]
    back = [X_MINUS, X_PLUS]
    tokens_bf = ((n_kv, length), BF)
    piece = ((n_kv, width // (NX * NZ)), BF)
    piece_f32 = (piece[0], F32)

    def columns(rows, step, half):
        start = (0, step, 0, half * half_width)
        return lax.dynamic_slice(rows, start, (1, 1, length, half_width))[0, 0]

    def swap_rows(rows, step, part):
        start = (0, step, part * length // 2, (1 - z_id) * half_width)
        away = lax.dynamic_slice(rows, start, (1, 1, length // 2, half_width))
        return send(away[0, 0], Z_SWAP)

    away = columns(inputs, 0, 1 - z_id)
    other = [send(away, Z_SWAP)]
    w_now = [value_w[0, f : f + n_kv] for f in firsts]
    token = jnp.zeros(*TOKEN)
    matrices = [None] * STEPS
    matrices[0], token = attention_matrices(away, token, queries, keys, inputs, 0)
    gathered = [gather_x(sides[c], w_now[c], token) for c in chunks]
    mine = columns(gated(inputs, token), 0, z_id)
    matrices[1], token = attention_matrices(away, token, queries, keys, inputs, 1)
    for step in range(STEPS):
        got, g_mine, g_other, opp_in, plain_in, added_in = ([None] * CHUNKS for _ in range(6))
        for c in chunks:
            (out,), token = ordered(
                value_body, "value_partial", x_id, token, [*gathered[c], *other], [tokens_bf]
            )
            got[c] = send(out, Z_SWAP)
        if step == 0:
            outer.send(token)
        for c in chunks:
            (g_mine[c],), token = ordered(
                functools.partial(grad_body, firsts[c] // HD),
                "grad_value",
                x_id,
                token,
                [*gathered[c], mine, got[c], *matrices[step]],
                [tokens_bf],
            )
            g_other[c] = send(g_mine[c], Z_SWAP)
        operands = [[g_mine[c], g_other[c], mine, *other] for c in chunks]
        for c in chunks:
            body = functools.partial(sum_body, sides[c])
            (opp, plain), token = ordered(body, "sum_partial", x_id, token, operands[c], [piece, piece])
            opp_in[c] = send(opp, there[c])
            plain_in[c] = send(plain, back[c])
        for c in chunks:
            body = functools.partial(add_body, sides[c])
            (added,), token = ordered(body, "sum_added", x_id, token, [*operands[c], opp_in[c]], [piece])
            added_in[c] = send(added, there[c])
        if step + 1 == STEPS:
            break
        outer.send(token)
        next_mine = columns(gated(inputs, token), step + 1, z_id)
        next_other = [swap_rows(gated(inputs, token), step + 1, 0)]
        for c in chunks:
            (w_now[c],), token = ordered(
                functools.partial(step_body, rate),
                "sum_step",
                x_id,
                token,
                [*operands[c], plain_in[c], added_in[c], w_now[c]],
                [piece],
            )
            gathered[c] = gather_x(sides[c], w_now[c])
        next_other.append(swap_rows(gated(inputs, token), step + 1, 1))
        mine, other = next_mine, next_other
    args = []
    for c in chunks:
        args += [g_mine[c], g_other[c], plain_in[c], added_in[c], w_now[c]]
    args += [mine, *other]
    both, momentum_out, anchor_out = next(outer)
    whole = ((1, *value_w.shape[1:]), BF)
    (value_out, delta_out), token = ordered(
        functools.partial(last_body, rate, CHUNKS), "last_step", x_id, token, [*args, both], [whole, whole]
    )
    return value_out, anchor_out, momentum_out, delta_out


def outer_stages(anchor, momentum, prev_delta):
    height, width = anchor.shape
    rep = lax.axis_index("rep")
    low = rep % 2 == 0
    along_y = [[r for r in range(N_REP) if r // 8 == g // 2 and r % 2 == g % 2] for g in range(8)]
    along_z = [[r for r in range(N_REP) if r % 8 == g] for g in range(8)]

    def gather(value, groups):
        return lax.all_gather(value, "rep", axis=0, axis_index_groups=groups)

    parts = prev_delta[0].reshape(NZH, NY, 2 * height, width).transpose(1, 0, 2, 3)
    sums = lax.psum_scatter(
        parts.reshape(N_REP * height, width),
        "rep",
        scatter_dimension=0,
        axis_index_groups=along_y,
        tiled=True,
    )
    owns = jnp.concatenate([anchor.astype(BF), momentum.astype(BF)], axis=0)
    token = yield
    rows = sums.shape[0]
    here = gated(jnp.concatenate([sums, owns], axis=0), token)
    there = lax.ppermute(here, "rep", [(r, r ^ 1) for r in range(N_REP)])
    sums = (here[:rows].astype(F32) + there[:rows].astype(F32)).astype(BF)
    first, second = jnp.where(low, here[rows:], there[rows:]), jnp.where(low, there[rows:], here[rows:])
    fill = jnp.zeros((2 * height, width), BF)
    near = gather(jnp.concatenate([sums, first, second, fill, fill], axis=0), along_z)
    token = yield
    near = gated(near, token)
    average = jnp.sum(near[:, :rows].astype(F32), axis=0) / N_REP
    owns = near[:, rows : rows + 4 * height].reshape(NZH, 2, 2, height, width).astype(F32)
    owns = owns.transpose(2, 0, 1, 3, 4).reshape(2, rows, width)
    momentum_new = outer_mu * owns[1] + average
    anchor_new = owns[0] - outer_rate * (outer_mu * momentum_new + average)
    both = gather(jnp.stack([anchor_new, owns[0]], axis=0).astype(BF), along_y)
    at = (rep // 8 * 2 + rep % 2) * height
    average = lax.dynamic_slice_in_dim(average, at, height, 0)
    momentum_out = outer_mu * momentum + average
    anchor_out = anchor - outer_rate * (outer_mu * momentum_out + average)
    yield
    yield both.reshape(NY, 2, NZH, 2 * height, width), momentum_out, anchor_out


def shards(inputs, queries, keys, value_w, anchor, momentum, prev_delta):
    outer = outer_stages(anchor, momentum, prev_delta)
    next(outer)
    return inner_steps(inputs, queries, keys, value_w, outer)


def solution(mesh):
    placed = (
        P("rep", None, "fsdp", None),
        P("rep", None, "fsdp", None),
        P("rep", None, "fsdp", None),
        P("rep", None, "fsdp"),
        P("rep", "fsdp"),
        P("rep", "fsdp"),
        P("rep", None, "fsdp"),
    )
    return jax.shard_map(
        shards,
        mesh=mesh,
        in_specs=placed,
        out_specs=(
            P("rep", None, "fsdp"),
            P("rep", "fsdp"),
            P("rep", "fsdp"),
            P("rep", None, "fsdp"),
        ),
        check_vma=False,
    )
```

```python
import functools
import math

import jax
import jax.numpy as jnp
from jax import lax
from jax.experimental import pallas as pl
from jax.experimental.pallas import tpu as pltpu
from jax.sharding import PartitionSpec as P

HD = 128
HQ = 32
KVH = 4
GROUP = HQ // KVH
STEPS = 2
CHUNKS = 2
NX = 4
NZ = 2

inner_rate = 0.5
outer_rate = 0.7
outer_mu = 0.9
mix_share = 0.5

BF = jnp.bfloat16
F32 = jnp.float32
NT = (((1,), (1,)), ((), ()))
NN = (((1,), (0,)), ((), ()))
VMEM_LIMIT = 16 * 1024 * 1024
ATTENTION_LIMIT = 60 * 1024 * 1024
TOKEN = ((8, 128), F32)
COST = pl.CostEstimate(flops=1000, bytes_accessed=1000, transcendentals=0)

X_PLUS = [(i, i // NX * NX + (i % NX + 1) % NX) for i in range(NX * NZ)]
X_MINUS = [(i, i // NX * NX + (i % NX + NX - 1) % NX) for i in range(NX * NZ)]
Z_SWAP = [(i, (i + NX) % (NX * NZ)) for i in range(NX * NZ)]
NY = 4
NZH = 4
N_REP = NZH * NY * 2


def dot(a, b, dims):
    return lax.dot_general(a, b, dims, preferred_element_type=F32)


def attention_kernel(_, t_in, q_ref, k_ref, x_ref, m_ref, nt_ref, t_out, w_low, w_high, targets):
    t_out[...] = t_in[...]
    length = k_ref.shape[0]
    half = length // 2
    k_low, k_high = k_ref[:half, :], k_ref[half:, :]
    u_at = lax.broadcasted_iota(jnp.int32, (half, half), 0)
    t_at = lax.broadcasted_iota(jnp.int32, (half, half), 1)
    keep = u_at <= t_at
    row_at = lax.broadcasted_iota(jnp.int32, (length, HD), 0)
    factor = math.log2(math.e) / math.sqrt(HD)
    for g in range(GROUP):
        cols = slice(g * HD, (g + 1) * HD)
        q_low, q_high = q_ref[:half, cols], q_ref[half:, cols]
        s_low = jnp.where(keep, dot(k_low, q_low, NT), -1e30)
        s_top = dot(k_low, q_high, NT)
        s_diag = jnp.where(keep, dot(k_high, q_high, NT), -1e30)
        peak = jnp.max(s_low, axis=0, keepdims=True)
        e_low = jnp.exp2((s_low - peak) * factor)
        w_low[:, cols] = (e_low * (1.0 / jnp.sum(e_low, axis=0, keepdims=True))).astype(BF)
        peak = jnp.max(jnp.maximum(s_top, s_diag), axis=0, keepdims=True)
        e_top = jnp.exp2((s_top - peak) * factor)
        e_diag = jnp.exp2((s_diag - peak) * factor)
        share = 1.0 / jnp.sum(e_top + e_diag, axis=0, keepdims=True)
        w_high[:half, cols] = (e_top * share).astype(BF)
        w_high[half:, cols] = (e_diag * share).astype(BF)
        shifted = pltpu.roll(x_ref[:, cols].astype(F32), length - 1, 0)
        target = jnp.where(row_at == length - 1, 0.0, shifted).astype(BF)
        targets[0, g * half : (g + 1) * half, :] = target[:half]
        targets[1, g * half : (g + 1) * half, :] = target[half:]
    m_high = dot(w_high[...], w_high[...], NT)
    m_low = dot(w_low[...], w_low[...], NT)
    m_ref[:half, :half] = (m_high[:half, :half] + m_low).astype(BF)
    m_ref[:half, half:] = m_high[:half, half:].astype(BF)
    m_ref[half:, :] = m_high[half:, :].astype(BF)
    n_high = dot(w_high[...], targets[1], NN)
    n_low = dot(w_low[...], targets[0], NN)
    nt_ref[:, :half] = (n_high[:half] + n_low).T
    nt_ref[:, half:] = n_high[half:].T


def attention_matrices(before, token, queries, keys, rows, step):
    length = rows.shape[2]
    half = length // 2
    wide = GROUP * HD
    m_part, nt_part, token = pl.pallas_call(
        attention_kernel,
        grid=(KVH,),
        in_specs=[
            pl.BlockSpec(memory_space=pl.ANY),
            pl.BlockSpec(TOKEN[0], lambda j: (0, 0)),
            pl.BlockSpec((None, None, length, wide), lambda j: (0, step, 0, j)),
            pl.BlockSpec((None, None, length, HD), lambda j: (0, step, 0, j)),
            pl.BlockSpec((None, None, length, wide), lambda j: (0, step, 0, j)),
        ],
        out_specs=[
            pl.BlockSpec((None, length, length), lambda j: (j, 0, 0)),
            pl.BlockSpec((HD, length), lambda j: (j, 0)),
            pl.BlockSpec(TOKEN[0], lambda j: (0, 0)),
        ],
        out_shape=[
            jax.ShapeDtypeStruct((KVH, length, length), BF),
            jax.ShapeDtypeStruct((KVH * HD, length), F32),
            jax.ShapeDtypeStruct(*TOKEN),
        ],
        scratch_shapes=[
            pltpu.VMEM((half, GROUP * half), BF),
            pltpu.VMEM((length, GROUP * half), BF),
            pltpu.VMEM((2, GROUP * half, HD), BF),
        ],
        compiler_params=pltpu.CompilerParams(vmem_limit_bytes=ATTENTION_LIMIT),
        cost_estimate=COST,
        name="attention_matrices",
    )(before, token, queries, keys, rows)
    return (m_part, nt_part), token


VMEM = pl.BlockSpec(memory_space=pltpu.VMEM)
SMEM = pl.BlockSpec(memory_space=pltpu.SMEM)


def ordered(body, name, x_id, token, operands, outs):
    def kernel(x_at, token_in, *refs):
        body(x_at[0], *refs[:-1])
        refs[-1][...] = token_in[...]

    results = pl.pallas_call(
        kernel,
        in_specs=[SMEM] + [VMEM] * (1 + len(operands)),
        out_specs=[VMEM] * (len(outs) + 1),
        out_shape=[jax.ShapeDtypeStruct(*o) for o in [*outs, TOKEN]],
        compiler_params=pltpu.CompilerParams(vmem_limit_bytes=VMEM_LIMIT),
        cost_estimate=COST,
        name=name,
    )(x_id, token, *operands)
    return results[:-1], results[-1]


def own_columns(x_id, k, width):
    return pl.ds(pl.multiple_of((x_id + k) % NX * width, width), width)


def value_piece(x_id, own, left, right, opp, rows):
    width = own.shape[1]
    acc = None
    for w_part, k in ((own, 0), (right, 1), (opp, 2), (left, 3)):
        term = dot(w_part[...], rows[:, own_columns(x_id, k, width)], NT)
        acc = term if acc is None else acc + term
    return acc


def value_body(x_id, own, left, right, opp, *refs):
    out, first = refs[-1], 0
    for other in refs[:-1]:
        cols = slice(first, first + other.shape[0])
        out[:, cols] = value_piece(x_id, own, left, right, opp, other).astype(BF)
        first = cols.stop


def grad_body(first, x_id, own, left, right, opp, mine, got, m_ref, nt_ref, out):
    value = value_piece(x_id, own, left, right, opp, mine)
    value = (value + got[...].astype(F32)).astype(BF)
    for j in range(out.shape[0] // HD):
        rows = slice(j * HD, (j + 1) * HD)
        at = first + j
        minus = nt_ref[at * HD : (at + 1) * HD, :]
        out[rows, :] = (dot(value[rows, :], m_ref[at], NN) - minus).astype(BF)


def sum_piece(x_id, k, width, g_mine, g_other, rows):
    cols = own_columns(x_id, k, width)
    total = dot(g_mine[...], rows[0][:, cols], NN)
    first = 0
    for other in rows[1:]:
        tokens = slice(first, first + other.shape[0])
        total = total + dot(g_other[:, tokens], other[:, cols], NN)
        first = tokens.stop
    return total


def sum_body(side, x_id, g_mine, g_other, *refs):
    *rows, opp, plain = refs
    width = opp.shape[1]
    for k, dst in ((2, opp), (4 - side, plain)):
        dst[...] = sum_piece(x_id, k, width, g_mine, g_other, rows).astype(BF)


def add_body(side, x_id, g_mine, g_other, *refs):
    *rows, opp_in, out = refs
    term = sum_piece(x_id, side, out.shape[1], g_mine, g_other, rows)
    out[...] = (term + opp_in[...].astype(F32)).astype(BF)


def step_body(rate, x_id, g_mine, g_other, *refs):
    *rows, plain_in, added_in, w_ref, out = refs
    total = sum_piece(x_id, 0, out.shape[1], g_mine, g_other, rows)
    total = total + plain_in[...].astype(F32) + added_in[...].astype(F32)
    out[...] = (w_ref[...].astype(F32) - rate * total).astype(BF)


def own_body(x_id, g_mine, g_other, *refs):
    *rows, out = refs
    out[...] = sum_piece(x_id, 0, out.shape[1], g_mine, g_other, rows)


def last_body(rate, n, x_id, *refs):
    *rows_refs, both, value_out, delta_out = refs[5 * n :]
    n_kv, (n_y, _, n_z, height, _) = value_out.shape[1] // n, both.shape
    near = [[both[y, i, z] for z in range(n_z) for y in range(n_y)] for i in (0, 1)]
    for c in range(n):
        g_mine, g_other, plain_in, added_in, w_ref = refs[5 * c : 5 * c + 5]
        total = sum_piece(x_id, 0, w_ref.shape[1], g_mine, g_other, rows_refs)
        total = total + plain_in[...].astype(F32) + added_in[...].astype(F32)
        inner = (w_ref[...].astype(F32) - rate * total).astype(BF).astype(F32)
        rows = slice(c * n_kv, (c + 1) * n_kv)
        here = slice(c * n_kv // height, (c + 1) * n_kv // height)
        new, old = (jnp.concatenate(v[here], axis=0).astype(F32) for v in near)
        value_out[0, rows, :] = (mix_share * inner + (1.0 - mix_share) * new).astype(BF)
        delta_out[0, rows, :] = (old - inner).astype(BF)


def send(value, perm):
    return lax.ppermute(value, "fsdp", perm)


def gather_x(side, own, gate=None):
    left = send(own, X_PLUS)
    right = send(own, X_MINUS)
    near, perm = (left, X_PLUS) if side == 1 else (right, X_MINUS)
    return own, left, right, send(near if gate is None else gated(near, gate), perm)


def gated(value, token):
    return lax.optimization_barrier((value, token))[0]


def inner_steps(inputs, queries, keys, value_w, outer):
    length, width = inputs.shape[2:]
    half_width = width // NZ
    at = lax.axis_index("fsdp")
    x_id = (at % NX).astype(jnp.int32).reshape(1)
    z_id = at // NX
    rate = inner_rate / (length * NX * NZ)
    n_kv = value_w.shape[1] // CHUNKS
    firsts = [c * n_kv for c in range(CHUNKS)]
    sides = [1, 3]
    chunks = range(CHUNKS)
    there = [X_PLUS, X_MINUS]
    back = [X_MINUS, X_PLUS]
    tokens_bf = ((n_kv, length), BF)
    piece = ((n_kv, width // (NX * NZ)), BF)
    piece_f32 = (piece[0], F32)

    def columns(rows, step, half):
        start = (0, step, 0, half * half_width)
        return lax.dynamic_slice(rows, start, (1, 1, length, half_width))[0, 0]

    def swap_rows(rows, step, part):
        start = (0, step, part * length // 2, (1 - z_id) * half_width)
        away = lax.dynamic_slice(rows, start, (1, 1, length // 2, half_width))
        return send(away[0, 0], Z_SWAP)

    away = columns(inputs, 0, 1 - z_id)
    other = [send(away, Z_SWAP)]
    w_now = [value_w[0, f : f + n_kv] for f in firsts]
    token = jnp.zeros(*TOKEN)
    matrices = [None] * STEPS
    matrices[0], token = attention_matrices(away, token, queries, keys, inputs, 0)
    gathered = [gather_x(sides[c], w_now[c], token) for c in chunks]
    mine = columns(gated(inputs, token), 0, z_id)
    matrices[1], token = attention_matrices(away, token, queries, keys, inputs, 1)
    for step in range(STEPS):
        got, g_mine, g_other, opp_in, plain_in, added_in = ([None] * CHUNKS for _ in range(6))
        for c in chunks:
            (out,), token = ordered(
                value_body, "value_partial", x_id, token, [*gathered[c], *other], [tokens_bf]
            )
            got[c] = send(out, Z_SWAP)
        if step == 0:
            outer.send(token)
        for c in chunks:
            (g_mine[c],), token = ordered(
                functools.partial(grad_body, firsts[c] // HD),
                "grad_value",
                x_id,
                token,
                [*gathered[c], mine, got[c], *matrices[step]],
                [tokens_bf],
            )
            g_other[c] = send(g_mine[c], Z_SWAP)
        operands = [[g_mine[c], g_other[c], mine, *other] for c in chunks]
        for c in chunks:
            body = functools.partial(sum_body, sides[c])
            (opp, plain), token = ordered(body, "sum_partial", x_id, token, operands[c], [piece, piece])
            opp_in[c] = send(opp, there[c])
            plain_in[c] = send(plain, back[c])
        if step + 1 < STEPS:
            next_mine = columns(gated(inputs, token), step + 1, z_id)
            next_other = [swap_rows(gated(inputs, token), step + 1, 0)]
        for c in chunks:
            body = functools.partial(add_body, sides[c])
            (added,), token = ordered(body, "sum_added", x_id, token, [*operands[c], opp_in[c]], [piece])
            added_in[c] = send(added, there[c])
        if step + 1 == STEPS:
            break
        outer.send(token)
        next_other.append(swap_rows(gated(inputs, token), step + 1, 1))
        for c in chunks:
            (w_now[c],), token = ordered(
                functools.partial(step_body, rate),
                "sum_step",
                x_id,
                token,
                [*operands[c], plain_in[c], added_in[c], w_now[c]],
                [piece],
            )
            gathered[c] = gather_x(sides[c], w_now[c])
        mine, other = next_mine, next_other
    args = []
    for c in chunks:
        args += [g_mine[c], g_other[c], plain_in[c], added_in[c], w_now[c]]
    args += [mine, *other]
    both, momentum_out, anchor_out = next(outer)
    whole = ((1, *value_w.shape[1:]), BF)
    (value_out, delta_out), token = ordered(
        functools.partial(last_body, rate, CHUNKS), "last_step", x_id, token, [*args, both], [whole, whole]
    )
    return value_out, anchor_out, momentum_out, delta_out


def outer_stages(anchor, momentum, prev_delta):
    height, width = anchor.shape
    rep = lax.axis_index("rep")
    low = rep % 2 == 0
    along_y = [[r for r in range(N_REP) if r // 8 == g // 2 and r % 2 == g % 2] for g in range(8)]
    along_z = [[r for r in range(N_REP) if r % 8 == g] for g in range(8)]

    def gather(value, groups):
        return lax.all_gather(value, "rep", axis=0, axis_index_groups=groups)

    parts = prev_delta[0].reshape(NZH, NY, 2 * height, width).transpose(1, 0, 2, 3)
    sums = lax.psum_scatter(
        parts.reshape(N_REP * height, width),
        "rep",
        scatter_dimension=0,
        axis_index_groups=along_y,
        tiled=True,
    )
    owns = jnp.concatenate([anchor, momentum], axis=0).astype(BF)
    token = yield
    rows = sums.shape[0]
    here = gated(jnp.concatenate([sums, owns], axis=0), token)
    there = lax.ppermute(here, "rep", [(r, r ^ 1) for r in range(N_REP)])
    sums = (here[:rows].astype(F32) + there[:rows].astype(F32)).astype(BF)
    first, second = jnp.where(low, here[rows:], there[rows:]), jnp.where(low, there[rows:], here[rows:])
    fill = jnp.zeros((2 * height, width), BF)
    near = gather(jnp.concatenate([sums, first, second, fill, fill], axis=0), along_z)
    token = yield
    near = gated(near, token)
    average = jnp.sum(near[:, :rows].astype(F32), axis=0) / N_REP
    owns = near[:, rows : rows + 4 * height].reshape(NZH, 2, 2, height, width).astype(F32)
    owns = owns.transpose(2, 0, 1, 3, 4).reshape(2, rows, width)
    momentum_new = outer_mu * owns[1] + average
    anchor_new = owns[0] - outer_rate * (outer_mu * momentum_new + average)
    both = gather(jnp.stack([anchor_new, owns[0]], axis=0).astype(BF), along_y)
    at = (rep // 8 * 2 + rep % 2) * height
    average = lax.dynamic_slice_in_dim(average, at, height, 0)
    momentum_out = outer_mu * momentum + average
    anchor_out = anchor - outer_rate * (outer_mu * momentum_out + average)
    yield
    yield both.reshape(NY, 2, NZH, 2 * height, width), momentum_out, anchor_out


def shards(inputs, queries, keys, value_w, anchor, momentum, prev_delta):
    outer = outer_stages(anchor, momentum, prev_delta)
    next(outer)
    return inner_steps(inputs, queries, keys, value_w, outer)


def solution(mesh):
    placed = (
        P("rep", None, "fsdp", None),
        P("rep", None, "fsdp", None),
        P("rep", None, "fsdp", None),
        P("rep", None, "fsdp"),
        P("rep", "fsdp"),
        P("rep", "fsdp"),
        P("rep", None, "fsdp"),
    )
    return jax.shard_map(
        shards,
        mesh=mesh,
        in_specs=placed,
        out_specs=(
            P("rep", None, "fsdp"),
            P("rep", "fsdp"),
            P("rep", "fsdp"),
            P("rep", None, "fsdp"),
        ),
        check_vma=False,
    )
```
